512 devices in a mesh: ctx: 8 (over x, core), vocab: 64 (over z, y).
Axes of the slice: x: 4, y: 8, z: 8, core: 2. Of those that a mesh axis runs over, the one named last changes fastest.
Arguments:
- hidden: bfloat16 [1024, 8192], P('ctx')
- head: bfloat16 [8192, 65536], P('ctx', 'vocab')
- targets: int32 [1024], P('ctx'), may hold values from 0 to 65535
- loss_mask: int32 [1024], P('ctx'), may hold values 0 or 1
- example_ids: int32 [1024], P('ctx'), may hold values from 0 to 1, never falling along the last dimension, each value on 1 to 768 neighbouring positions
- down_input: bfloat16 [1024, 28672], P('ctx', 'vocab'), may hold values from -6 to 6
- proj_hidden: bfloat16 [8192, 64], P('ctx'), may hold values from -0.0625 to 0.0625
- proj_vocab: bfloat16 [65536, 64], P('vocab'), may hold values from -6 to 6
- proj_grad: bfloat16 [8192, 64], P('ctx'), may hold values from -1.5 to 1.5
- proj_act: bfloat16 [28672, 64], P('vocab'), may hold values from -0.03125 to 0.03125
Outputs:
- head_features: float32 [2, 4096], replicated
- down_features: float32 [2, 4096], replicated
The draws below stay inside these ranges and needn't reach their ends.
Inputs may be any that keep to these rules, and one draw needn't show every extreme that they name: `example_ids`: example numbers never fall along the tokens; each example has 1 to 768 tokens.
All inputs are finite; a program needn't handle non-finite values. No bound on the sum of `loss_mask` on one device may be relied on, other than what follows from the above.
Results may differ from the reference program's by a relative error of at most 0.0015.
Values may be sent and summed in bfloat16 or wider, within the bound.
A program may use at most 64 MiB of HBM per device.

```python
import math
import jax
import jax.numpy as jnp
import numpy as np
from jax import lax

D = 8192
FF = 28672
RANK = 64
EXAMPLES = 2
VOCAB = 65536
TOKENS = 1024
MOST = 768


logit_spread = 4.0


def head_column(key, column_index, column_size):
    column_key = jax.random.fold_in(jax.random.fold_in(key, 7), column_index)
    return jax.random.normal(column_key, (column_size,), jnp.float32)


def draw_head(key, part):
    columns = jax.vmap(lambda column_index: head_column(key, column_index, D))(jnp.arange(VOCAB))
    return (columns.T * (logit_spread * D ** (-0.5))).astype(jnp.bfloat16)


def draw_hidden(key, part):
    key = jax.random.fold_in(key, 3)
    noise_key = jax.random.fold_in(key, 0)
    values = jnp.clip(jax.random.normal(noise_key, (TOKENS, D), jnp.float32), -6.0, 6.0)
    return values.astype(jnp.bfloat16)


def place_ends(values, stream_key, least, top_value):
    index_at = [jax.random.randint(jax.random.fold_in(stream_key, axis), (), 0, length) for axis, length in enumerate(values.shape)]
    longest = values.shape.index(max(values.shape))
    next_to = index_at[:longest] + [(index_at[longest] + 1) % values.shape[longest]] + index_at[longest + 1:]
    return values.at[tuple(index_at)].set(least).at[tuple(next_to)].set(top_value)


def block_scale(rng, dims, cuts, low, top_value):
    def one(axis_at, parts):
        heights = jax.random.uniform(jax.random.fold_in(jax.random.fold_in(rng, 6), axis_at), (parts,), jnp.float32, low / len(cuts), top_value / len(cuts))
        return jnp.repeat(jnp.exp(heights), dims[axis_at] // parts).reshape((-1,) + (1,) * (len(dims) - axis_at - 1))

    level = one(*cuts[0])
    for cut in cuts[1:]:
        level = level * one(*cut)
    return level


def rank_bounds(number_of, skew):
    loads = [(1 << 20) // math.isqrt(rank ** skew) + 1 for rank in range(1, number_of + 1)]
    spread = 1 + sum(loads) // (1 << 30)
    return np.cumsum(np.array([max(1, weight // spread) for weight in loads]))


def skewed_ids(stream_key, shape, number_of, lean):
    grid = rank_bounds(number_of, lean)
    pick = jax.random.randint(jax.random.fold_in(stream_key, 1), shape, 0, int(grid[number_of - 1]))
    grade = jnp.searchsorted(jnp.asarray(grid, jnp.int32), pick, side="right")
    return jax.random.permutation(jax.random.fold_in(stream_key, 2), number_of)[grade].astype(jnp.int32)


def length_profile(number_of, total, bound, slope):
    portions = [(1 << 20) // math.isqrt(standing ** slope) + 1 for standing in range(2, number_of + 1)]
    rest, holding = total - bound - (number_of - 1), [1] * (number_of - 1)
    while rest > 0:
        candidates = [i for i in range(number_of - 1) if holding[i] < bound]
        whole, left = sum([portions[i] for i in candidates]), rest
        for i in candidates:
            extra = min(bound - holding[i], max(1, left * portions[i] // whole), rest)
            holding[i] = holding[i] + extra
            rest = rest - extra
    return np.array([bound] + holding)


def uneven(rng, number_of, total, bound, skew):
    if number_of == 2:
        one = jax.random.randint(rng, (), max(1, total - bound), min(bound, total - 1) + 1)
        return jnp.stack([one, total - one])
    tallies = jnp.asarray(length_profile(number_of, total, bound, skew), jnp.int32)
    couples = (number_of - 1) // 2
    source_of, taker = tallies[1:1 + 2 * couples:2], tallies[2:2 + 2 * couples:2]
    room = jnp.minimum(source_of - 1, bound - taker)
    moved = jax.random.randint(jax.random.fold_in(rng, 1), (couples,), 0, 1 << 20) % (room + 1)
    tallies = tallies.at[1:1 + 2 * couples:2].set(source_of - moved).at[2:2 + 2 * couples:2].set(taker + moved)
    return tallies[jax.random.permutation(jax.random.fold_in(rng, 2), number_of)]


def scatter_about(own_key, extent, deviation, limit, cuts=(), held_as=jnp.bfloat16):
    values = deviation * jax.random.normal(own_key, extent, jnp.float32)
    if cuts:
        values = values * block_scale(own_key, extent, cuts, -0.22, 0.18)
    return jnp.clip(values, -limit, limit).astype(held_as)


def setup_inputs(seed: int = 0) -> dict:
    key_list = jax.random.split(jax.random.key(seed), 11)
    return {
        "hidden": draw_hidden(jax.random.fold_in(key_list[10], 71), 0),
        "head": draw_head(jax.random.fold_in(key_list[10], 71), 0),
        "targets": place_ends(skewed_ids(key_list[2], (TOKENS,), VOCAB, 2), jax.random.fold_in(key_list[2], 3), 0, VOCAB - 1).astype(jnp.int32),
        "loss_mask": place_ends((jax.random.randint(key_list[3], (TOKENS,), 0, 8) < 7).astype(jnp.int32), jax.random.fold_in(key_list[3], 1), 0, 1),
        "example_ids": jnp.searchsorted(jnp.cumsum(uneven(key_list[4], EXAMPLES, TOKENS, MOST, 2)), jnp.arange(TOKENS), side="right").astype(jnp.int32),
        "down_input": scatter_about(key_list[5], (TOKENS, FF), 1.0, 6.0, ((0, 8), (1, 64))),
        "proj_hidden": scatter_about(key_list[6], (D, RANK), D ** -0.5, 0.0625, ((0, 8),)),
        "proj_vocab": scatter_about(key_list[7], (VOCAB, RANK), 1.0, 6.0, ((0, 64),)),
        "proj_grad": scatter_about(key_list[8], (D, RANK), 0.25, 1.5, ((0, 8),)),
        "proj_act": scatter_about(key_list[9], (FF, RANK), FF ** -0.5, 0.03125, ((0, 64),)),
    }


def reference(hidden, head, targets, loss_mask, example_ids, down_input, proj_hidden, proj_vocab, proj_grad, proj_act):
    logits = jnp.dot(hidden, head, preferred_element_type=jnp.float32)
    row_top = jnp.max(logits, axis=1, keepdims=True)
    shifted = jnp.exp(logits - row_top)
    row_total = jnp.sum(shifted, axis=1, keepdims=True)
    column_ids = jnp.arange(VOCAB, dtype=jnp.int32)
    onehot = (targets[:, None] == column_ids[None, :]).astype(jnp.float32)
    weights_mask = loss_mask.astype(jnp.float32)[:, None]
    token_grad = (weights_mask * (shifted / row_total - onehot)).astype(jnp.bfloat16)
    hidden_proj = jnp.dot(hidden, proj_hidden, preferred_element_type=jnp.float32)
    act_proj = jnp.dot(down_input, proj_act, preferred_element_type=jnp.float32)
    grad_proj = jnp.dot(token_grad, proj_vocab, preferred_element_type=jnp.float32)
    grad_basis = lax.dot_general(proj_grad, head, (((0,), (0,)), ((), ())), preferred_element_type=jnp.float32)
    down_proj = lax.dot_general(token_grad.astype(jnp.float32), grad_basis, (((1,), (1,)), ((), ())), precision=lax.Precision.HIGHEST)
    membership = (example_ids[None, :] == jnp.arange(EXAMPLES, dtype=jnp.int32)[:, None]).astype(jnp.float32)
    factor = TOKENS ** -0.5
    outer_head = (hidden_proj[:, :, None] * grad_proj[:, None, :]).reshape(TOKENS, RANK * RANK)
    outer_down = (act_proj[:, :, None] * down_proj[:, None, :]).reshape(TOKENS, RANK * RANK)
    head_features = factor * jnp.dot(membership, outer_head, precision=lax.Precision.HIGHEST)
    down_features = factor * jnp.dot(membership, outer_down, precision=lax.Precision.HIGHEST)
    return head_features, down_features
```

```python
import functools

import jax
import jax.numpy as jnp
from jax import lax
from jax.experimental import pallas as pl
from jax.experimental.pallas import tpu as pltpu
from jax.sharding import PartitionSpec as P

MESH = pl.DeviceIdType.MESH
NX, NC, NY, NZ = 4, 2, 8, 8
EXAMPLES = 2
COPIES = 67
NT = (((1,), (1,)), ((), ()))
TN = (((0,), (0,)), ((), ()))
F32, BF16 = jnp.float32, jnp.bfloat16


def kernel(
    hidden, head, ids, down_input, ph, pv, pg, pa,
    out,
    heads, hid, fwd, pgs, phs, gpart, grecv, gfull, hps, hrecv,
    part, recv_a, recv_b, w, vy, ry, vz, rz, mz, az, my, ay, feat, rc, mc, fa,
    lsem, ssem, rsem,
):
    i, j = lax.axis_index("ctx"), lax.axis_index("vocab")
    x, c = i // NC, i % NC
    z, y = j // NY, j % NY

    def peer(dx=0, dc=0, dy=0, dz=0):
        return (
            ((x + dx) % NX) * NC + (c + dc) % NC,
            ((z + dz) % NZ) * NY + (y + dy) % NY,
        )

    ctx_peers = [(dx, dc) for dx in range(NX) for dc in range(NC) if dx or dc]
    started = []

    def send(src, dst, to):
        k = len(started)
        copy = pltpu.make_async_remote_copy(
            src_ref=src, dst_ref=dst, send_sem=ssem.at[k], recv_sem=rsem.at[k],
            device_id=to, device_id_type=MESH,
        )
        copy.start()
        started.append(copy)
        return copy

    def dot(a, b, dims=NT):
        return lax.dot_general(a, b, dims, preferred_element_type=F32)

    dm = heads.shape[1]
    wide = NC * dm
    vc = heads.shape[2]
    half = vc // 2
    rows = hid.shape[1]
    low = lax.broadcasted_iota(jnp.int32, (1, 128), 1) < 64

    def columns_of(chip):
        return pl.ds(pl.multiple_of(chip * wide, 128), wide)

    own_head = pltpu.make_async_copy(head, heads.at[c], lsem.at[0])
    own_head.start()
    own_hid = pltpu.make_async_copy(hidden.at[:, columns_of(x)], hid.at[x], lsem.at[1])
    own_hid.start()

    barrier = pltpu.get_barrier_semaphore()
    for dx, dc in ctx_peers:
        pl.semaphore_signal(barrier, inc=1, device_id=peer(dx, dc), device_id_type=MESH)
    for d in range(1, NY):
        pl.semaphore_signal(barrier, inc=1, device_id=peer(dy=d), device_id_type=MESH)
    for d in range(1, NZ):
        pl.semaphore_signal(barrier, inc=1, device_id=peer(dz=d), device_id_type=MESH)
    pl.semaphore_wait(barrier, len(ctx_peers) + NY - 1 + NZ - 1)

    right, left = peer(dx=1), peer(dx=NX - 1)
    sibling = peer(dc=1)
    xr, xl, xo = (x + 1) % NX, (x + NX - 1) % NX, (x + 2) % NX

    hr = rows // 2
    to_opp_r = send(hidden.at[pl.ds(0, hr), columns_of(xo)], fwd.at[0], right)
    to_opp_l = send(hidden.at[pl.ds(hr, hr), columns_of(xo)], fwd.at[1], left)
    head_copy = send(head, heads.at[c], sibling)
    pg_copy = send(pg, pgs.at[c], sibling)
    ph_copy = send(ph, phs.at[c], sibling)
    hid_r = send(hidden.at[:, columns_of(xr)], hid.at[x], right)
    hid_l = send(hidden.at[:, columns_of(xl)], hid.at[x], left)

    pgs[c] = pg[...]
    phs[c] = ph[...]

    act_t = dot(pa[...], down_input[...], (((1,), (0,)), ((), ())))
    act = jnp.concatenate([act_t, act_t], axis=0).T

    to_opp_r.wait_recv()
    fwd_r = send(fwd.at[0], hid.at[xl, pl.ds(0, hr)], right)
    to_opp_l.wait_recv()
    fwd_l = send(fwd.at[1], hid.at[xr, pl.ds(hr, hr)], left)

    own_head.wait()
    head_copy.wait_recv()
    pg_copy.wait_recv()
    quarter = vc // NX
    for q in range(NX):
        cols = pl.ds(q * quarter, quarter)
        gpart[q] = sum(
            dot(pgs[k], heads[k, :, cols], (((1,), (0,)), ((), ()))) for k in range(NC)
        )
    hr64 = gpart.shape[1] // NC
    mine = pl.ds(pl.multiple_of(c * hr64, 8), hr64)
    g_sum = [
        send(gpart.at[(x + d) % NX, mine], grecv.at[d - 1], peer(dx=d)) for d in range(1, NX)
    ]
    ph_copy.wait_recv()

    def logits(chip, slot, h):
        cols = pl.ds(h * half, half)
        part[slot, h] = sum(
            dot(
                hid[chip, :, k * dm : (k + 1) * dm], heads[k, :, cols],
                (((1,), (0,)), ((), ())),
            )
            for k in range(NC)
        )

    def project(chip):
        hp = sum(dot(hid[chip, :, k * dm : (k + 1) * dm], phs[k]) for k in range(NC))
        hps[chip] = jnp.concatenate([hp, hp], axis=1)

    own_hid.wait()
    for h in range(2):
        logits(x, 3, h)
    project(x)

    for copy in g_sum:
        copy.wait_recv()
    gfull[x, mine] = gpart[x, mine] + grecv[0] + grecv[1] + grecv[2]
    g_all = [
        send(gfull.at[x, mine], gfull.at[x, mine], peer(dx=d)) for d in range(1, NX)
    ]

    owner = NZ * y + z
    group = pl.ds(pl.multiple_of((owner // 4) * 8, 8), 8)

    hid_r.wait_recv()
    logits(xl, 2, 0)
    s_l0 = send(part.at[2, 0], recv_b.at[1, 0], left)
    logits(xl, 2, 1)
    hid_l.wait_recv()
    logits(xr, 1, 1)
    s_r1 = send(part.at[1, 1], recv_b.at[0, 1], right)
    logits(xr, 1, 0)
    fwd_r.wait_recv()
    fwd_l.wait_recv()
    logits(xo, 0, 0)
    a_r = send(part.at[0, 0], recv_a.at[0], right)
    logits(xo, 0, 1)
    a_l = send(part.at[0, 1], recv_a.at[1], left)

    for chip in (xl, xr, xo):
        project(chip)
    hp_sum = [
        send(hps.at[(x + d) % NX, group], hrecv.at[d - 1], peer(dx=d)) for d in range(1, NX)
    ]

    a_r.wait_recv()
    part[1, 0] = part[1, 0] + recv_a[0]
    s_r0 = send(part.at[1, 0], recv_b.at[0, 0], right)
    a_l.wait_recv()
    part[2, 1] = part[2, 1] + recv_a[1]
    s_l1 = send(part.at[2, 1], recv_b.at[1, 1], left)

    for copy in g_all:
        copy.wait_recv()
    g_sib = send(gfull.at[:, mine], gfull.at[:, mine], sibling)
    g_sib.wait_recv()
    for q in range(NX):
        cols = pl.ds(q * quarter, quarter)
        g = gfull[q]
        high = g.astype(BF16)
        w[0:64, cols] = pv[:, cols]
        w[64:128, cols] = high
        w[128:192, cols] = jnp.zeros_like(high)
        w[192:256, cols] = (g - high.astype(F32)).astype(BF16)

    id_cols = [jnp.broadcast_to(ids[k : k + 1, :], (rows, rows)).T for k in range(3)]
    target = id_cols[0][:, 0:1]

    for copy in (s_l0, s_r1, s_r0, s_l1):
        copy.wait_recv()
    vals = [part[3, h] + recv_b[0, h] + recv_b[1, h] for h in range(2)]
    top = jnp.maximum(
        jnp.max(vals[0], axis=1, keepdims=True), jnp.max(vals[1], axis=1, keepdims=True)
    )
    total = jnp.zeros_like(top)
    acc = jnp.zeros((3 * rows, 256), F32)
    for h in range(2):
        e = jnp.exp(vals[h] - top)
        total = total + jnp.sum(e, axis=1, keepdims=True)
        e_high = e.astype(BF16)
        e_low = (e - e_high.astype(F32)).astype(BF16)
        ids_here = lax.broadcasted_iota(jnp.int32, (rows, half), 1) + (j * vc + h * half)
        onehot = jnp.where(ids_here == target, 1.0, 0.0).astype(BF16)
        lhs = jnp.concatenate([e_high, e_low, onehot], axis=0)
        acc = acc + dot(lhs, w[:, h * half : (h + 1) * half])
    both = acc[:, 0:128] + acc[:, 128:256]

    per = 4
    vy[pl.ds(0, rows, stride=per), :] = both[0:rows] + both[rows : 2 * rows]
    vy[pl.ds(1, rows, stride=per), :] = both[2 * rows :]
    vy[pl.ds(2, rows, stride=per), :] = jnp.where(low, act, total)
    vy[pl.ds(3, rows, stride=per), :] = jnp.broadcast_to(top, (rows, 128))

    chunk = vy.shape[0] // NY
    got = [
        send(vy.at[pl.ds(pl.multiple_of(((y + d) % NY) * chunk, 8), chunk)], ry.at[d], peer(dy=d))
        for d in range(1, NY)
    ]
    ry[0] = vy[pl.ds(pl.multiple_of(y * chunk, 8), chunk), :]
    for copy in got:
        copy.wait_recv()
    n = chunk // per
    tops = [ry[d, pl.ds(3, n, stride=per), :] for d in range(NY)]
    best = functools.reduce(jnp.maximum, tops)
    scale = [jnp.exp(t - best) for t in tops]
    mixed = [ry[d, pl.ds(2, n, stride=per), :] for d in range(NY)]
    vz[pl.ds(0, n, stride=per), :] = sum(
        scale[d] * ry[d, pl.ds(0, n, stride=per), :] for d in range(NY)
    )
    vz[pl.ds(1, n, stride=per), :] = sum(ry[d, pl.ds(1, n, stride=per), :] for d in range(NY))
    vz[pl.ds(2, n, stride=per), :] = sum(
        jnp.where(low, mixed[d], mixed[d] * scale[d]) for d in range(NY)
    )
    vz[pl.ds(3, n, stride=per), :] = best

    got = [
        send(vz.at[pl.ds(pl.multiple_of(((z + d) % NZ) * 8, 8), 8)], rz.at[pl.ds(8 * d, 8)], peer(dz=d))
        for d in range(1, NZ)
    ]
    rz[0:8, :] = vz[pl.ds(pl.multiple_of(z * 8, 8), 8), :]
    for copy in hp_sum:
        copy.wait_recv()
    hp_rows = hps[x, group, :] + hrecv[0] + hrecv[1] + hrecv[2]
    row_ids = lax.broadcasted_iota(jnp.int32, (8, 1), 0)
    for copy in got:
        copy.wait_recv()
    mz[...] = jnp.zeros_like(mz)
    for t in range(2):
        at = [rz[pl.ds(4 * t + k, NZ, stride=8), :] for k in range(4)]
        best = jnp.max(at[3], axis=0, keepdims=True)
        scale = jnp.exp(at[3] - best)
        soft = jnp.sum(scale * at[0], axis=0, keepdims=True)
        hot = jnp.sum(at[1], axis=0, keepdims=True)
        mix = jnp.sum(jnp.where(low, at[2], at[2] * scale), axis=0, keepdims=True)
        denominator = jnp.where(low, pltpu.roll(mix, 64, 1), mix)
        hp = jnp.sum(
            jnp.where(row_ids == 2 * (owner % 4) + t, hp_rows, 0.0), axis=0, keepdims=True
        )
        mz[4 * t : 4 * t + 1, :] = soft / denominator - hot
        mz[4 * t + 1 : 4 * t + 2, :] = jnp.where(low, mix, hp)

    got = [send(mz, az.at[pl.ds(pl.multiple_of(8 * z, 8), 8)], peer(dz=d)) for d in range(1, NZ)]
    az[pl.ds(pl.multiple_of(8 * z, 8), 8), :] = mz[...]
    for copy in got:
        copy.wait_recv()
    for k in range(2):
        my[k * n : (k + 1) * n, :] = az[pl.ds(k, n, stride=per), :]

    got = [send(my, ay.at[y], peer(dy=d)) for d in range(1, NY)]
    ay[y] = my[...]
    for copy in got:
        copy.wait_recv()
    grads = jnp.concatenate([ay[d, 0:n] for d in range(NY)], axis=0)
    feats = jnp.concatenate([ay[d, n : 2 * n] for d in range(NY)], axis=0)
    factor = (rows * NX * NC) ** -0.5
    grads = grads * (id_cols[1].astype(F32) * factor)
    lhs = jnp.concatenate(
        [jnp.where(id_cols[2] == e, feats, 0.0) for e in range(EXAMPLES)], axis=1
    )
    outer = lax.dot_general(
        lhs, grads, TN, precision=lax.Precision.HIGHEST, preferred_element_type=F32
    )
    for e in range(EXAMPLES):
        feat[64 * e : 64 * e + 64, :] = jnp.where(
            low, outer[128 * e + 64 : 128 * e + 128], outer[128 * e : 128 * e + 64]
        )

    span = feat.shape[0] // (NX * NC)
    got = [
        send(
            feat.at[pl.ds(pl.multiple_of(peer(dx, dc)[0] * span, 8), span)],
            rc.at[k], peer(dx, dc),
        )
        for k, (dx, dc) in enumerate(ctx_peers)
    ]
    own = feat[pl.ds(pl.multiple_of(i * span, 8), span), :]
    for copy in got:
        copy.wait_recv()
    mc[...] = own + sum(rc[k] for k in range(len(ctx_peers)))
    got = [send(mc, fa.at[pl.ds(pl.multiple_of(i * span, 8), span)], peer(dx, dc)) for dx, dc in ctx_peers]
    fa[pl.ds(pl.multiple_of(i * span, 8), span), :] = mc[...]
    for copy in got:
        copy.wait_recv()
    m = 32
    for e in range(EXAMPLES):
        even = fa[pl.ds(64 * e, m, stride=2), :]
        odd = fa[pl.ds(64 * e + 1, m, stride=2), :]
        out[0, e] = jnp.where(low, even, pltpu.roll(odd, 64, 1))
        out[1, e] = jnp.where(low, pltpu.roll(even, 64, 1), odd)

    for copy in started:
        copy.wait_send()


def local(
    hidden, head, targets, loss_mask, example_ids, down_input, proj_hidden, proj_vocab, proj_grad,
    proj_act,
):
    rows = hidden.shape[0]
    dm, vc = head.shape
    rank = proj_hidden.shape[1]
    half, quarter = vc // 2, vc // NX
    ids = jnp.stack([targets, loss_mask, example_ids])
    vmem = pl.BlockSpec(memory_space=pltpu.VMEM)
    anywhere = pl.BlockSpec(memory_space=pl.ANY)
    out = pl.pallas_call(
        kernel,
        out_shape=jax.ShapeDtypeStruct((2, EXAMPLES, 32, 128), F32),
        in_specs=[anywhere, anywhere] + [vmem] * 6,
        out_specs=vmem,
        scratch_shapes=[
            pltpu.VMEM((NC, dm, vc), BF16),
            pltpu.VMEM((NX, rows, NC * dm), BF16),
            pltpu.VMEM((2, rows // 2, NC * dm), BF16),
            pltpu.VMEM((NC, rank, dm), BF16),
            pltpu.VMEM((NC, rank, dm), BF16),
            pltpu.VMEM((NX, rank, quarter), F32),
            pltpu.VMEM((NX - 1, rank // NC, quarter), F32),
            pltpu.VMEM((NX, rank, quarter), F32),
            pltpu.VMEM((NX, rows, 128), F32),
            pltpu.VMEM((NX - 1, 8, 128), F32),
            pltpu.VMEM((4, 2, rows, half), F32),
            pltpu.VMEM((2, rows, half), F32),
            pltpu.VMEM((2, 2, rows, half), F32),
            pltpu.VMEM((256, vc), BF16),
            pltpu.VMEM((4 * rows, 128), F32),
            pltpu.VMEM((NY, 4 * rows // NY, 128), F32),
            pltpu.VMEM((8 * NZ, 128), F32),
            pltpu.VMEM((8 * NZ, 128), F32),
            pltpu.VMEM((8, 128), F32),
            pltpu.VMEM((8 * NZ, 128), F32),
            pltpu.VMEM((4 * NZ, 128), F32),
            pltpu.VMEM((NY, 4 * NZ, 128), F32),
            pltpu.VMEM((64 * EXAMPLES, 128), F32),
            pltpu.VMEM((NX * NC - 1, 16, 128), F32),
            pltpu.VMEM((16, 128), F32),
            pltpu.VMEM((64 * EXAMPLES, 128), F32),
            pltpu.SemaphoreType.DMA((2,)),
            pltpu.SemaphoreType.DMA((COPIES,)),
            pltpu.SemaphoreType.DMA((COPIES,)),
        ],
        compiler_params=pltpu.CompilerParams(
            collective_id=0, has_side_effects=True, vmem_limit_bytes=48 * 2**20
        ),
        name="features",
    )(
        hidden, head, ids, down_input.T, proj_hidden.T, proj_vocab.T, proj_grad.T, proj_act.T
    )
    return out[0].reshape(EXAMPLES, rank * rank), out[1].reshape(EXAMPLES, rank * rank)


def solution(mesh):
    return jax.shard_map(
        local,
        mesh=mesh,
        in_specs=(
            P("ctx", None),
            P("ctx", "vocab"),
            P("ctx"),
            P("ctx"),
            P("ctx"),
            P("ctx", "vocab"),
            P("ctx", None),
            P("vocab", None),
            P("ctx", None),
            P("vocab", None),
        ),
        out_specs=(P(), P()),
        check_vma=False,
    )
```

```python
import functools

import jax
import jax.numpy as jnp
from jax import lax
from jax.experimental import pallas as pl
from jax.experimental.pallas import tpu as pltpu
from jax.sharding import PartitionSpec as P

MESH = pl.DeviceIdType.MESH
NX, NC, NY, NZ = 4, 2, 8, 8
EXAMPLES = 2
COPIES = 88
NT = (((1,), (1,)), ((), ()))
TN = (((0,), (0,)), ((), ()))
F32, BF16 = jnp.float32, jnp.bfloat16


def kernel(
    hidden, head, targets, mask, examples, down_input, ph, pv, pg, pa,
    out,
    ids, di, pac, heads, hid, pgs, phs, gpart, grecv, gfull, hps, hrecv,
    part, recv_a, recv_b, w, ve, re, vz, rz, be, vy, ry, vf, rf, my, ay, feat, rc, whole,
    lsem, ssem, rsem,
):
    i, j = lax.axis_index("ctx"), lax.axis_index("vocab")
    x, c = i // NC, i % NC
    z, y = j // NY, j % NY

    def peer(dx=0, dc=0, dy=0, dz=0):
        return (
            ((x + dx) % NX) * NC + (c + dc) % NC,
            ((z + dz) % NZ) * NY + (y + dy) % NY,
        )

    ctx_peers = [(dx, dc) for dx in range(NX) for dc in range(NC) if dx or dc]
    started = []

    def send(src, dst, to):
        k = len(started)
        copy = pltpu.make_async_remote_copy(
            src_ref=src, dst_ref=dst, send_sem=ssem.at[k], recv_sem=rsem.at[k],
            device_id=to, device_id_type=MESH,
        )
        copy.start()
        started.append(copy)
        return copy

    def dot(a, b, dims=NT):
        return lax.dot_general(a, b, dims, preferred_element_type=F32)

    dm = heads.shape[1]
    wide = NC * dm
    vc = heads.shape[2]
    half = vc // 2
    rows = hid.shape[1]
    few = rows // NY
    low = lax.broadcasted_iota(jnp.int32, (1, 128), 1) < 64

    def columns_of(chip):
        return pl.ds(pl.multiple_of(chip * wide, 128), wide)

    loads = [
        pltpu.make_async_copy(src, dst, lsem.at[k])
        for k, (src, dst) in enumerate([
            (head, heads.at[c]),
            (hidden.at[:, columns_of(x)], hid.at[x]),
            (pg, pgs.at[c]),
            (ph, phs.at[c]),
            (pv, w.at[pl.ds(0, 64)]),
            (down_input, di),
            (pa, pac),
            (targets, ids.at[0]),
            (mask, ids.at[1]),
            (examples, ids.at[2]),
        ])
    ]
    for copy in loads:
        copy.start()
    own_head, own_hid, own_pg, own_ph, own_pv, own_di, own_pa = loads[:7]

    barrier = pltpu.get_barrier_semaphore()
    for dx, dc in ctx_peers:
        pl.semaphore_signal(barrier, inc=1, device_id=peer(dx, dc), device_id_type=MESH)
    for d in range(1, NY):
        pl.semaphore_signal(barrier, inc=1, device_id=peer(dy=d), device_id_type=MESH)
    for d in range(1, NZ):
        pl.semaphore_signal(barrier, inc=1, device_id=peer(dz=d), device_id_type=MESH)
    pl.semaphore_wait(barrier, len(ctx_peers) + NY - 1 + NZ - 1)

    right, left = peer(dx=1), peer(dx=NX - 1)
    up, down = peer(dy=1), peer(dy=NY - 1)
    sibling = peer(dc=1)
    xr, xl, xo = (x + 1) % NX, (x + NX - 1) % NX, (x + 2) % NX

    def slab(chip, dy, piece=None):
        at = pl.ds(pl.multiple_of(((y + dy) % NY) * few, few), few)
        if piece is None:
            return hid.at[chip, at]
        return hid.at[chip, at, pl.ds(piece * dm, dm)]

    my_rows = pl.ds(pl.multiple_of(y * few, few), few)
    shares = [
        send(hidden.at[my_rows, columns_of((x + d) % NX)], hid.at[x, my_rows], peer(dx=d))
        for d in (2, 1, 3)
    ]
    blocks = (xo, xl, xr)
    head_copy = send(head, heads.at[c], sibling)
    pg_copy = send(pg, pgs.at[c], sibling)
    ph_copy = send(ph, phs.at[c], sibling)

    def both_ways(arrived, dy, pieces=(None, None)):
        moved = []
        for (from_down, from_up), chip in zip(arrived, blocks):
            from_down.wait_recv()
            going_up = slab(chip, -dy, pieces[0])
            moved_up = send(going_up, going_up, up)
            if from_up is not from_down:
                from_up.wait_recv()
            going_down = slab(chip, dy, pieces[1])
            moved.append((moved_up, send(going_down, going_down, down)))
        return moved

    hops = both_ways([(copy, copy) for copy in shares], 0)

    own_di.wait()
    own_pa.wait()
    act_t = dot(pac[...], di[...], (((1,), (0,)), ((), ())))
    act = jnp.concatenate([act_t, act_t], axis=0).T
    for d in range(NY):
        ve[d, few : 2 * few] = act[d * few : (d + 1) * few]

    own_head.wait()
    own_pg.wait()
    head_copy.wait_recv()
    pg_copy.wait_recv()
    hops = both_ways(hops, 1)
    quarter = vc // NX
    for q in range(NX):
        cols = pl.ds(q * quarter, quarter)
        gpart[q] = sum(
            dot(pgs[k], heads[k, :, cols], (((1,), (0,)), ((), ()))) for k in range(NC)
        )
    share = gpart.shape[1] // NC
    mine = pl.ds(pl.multiple_of(c * share, 8), share)
    g_sum = [
        send(gpart.at[(x + d) % NX, mine], grecv.at[d - 1], peer(dx=d)) for d in range(1, NX)
    ]

    def logits(chip, slot, h):
        cols = pl.ds(h * half, half)
        part[slot, h] = sum(
            dot(
                hid[chip, :, k * dm : (k + 1) * dm], heads[k, :, cols],
                (((1,), (0,)), ((), ())),
            )
            for k in range(NC)
        )

    def project(chip):
        hp = sum(dot(hid[chip, :, k * dm : (k + 1) * dm], phs[k]) for k in range(NC))
        hps[chip] = jnp.concatenate([hp, hp], axis=1)

    own_hid.wait()
    hops = both_ways(hops, 2)
    for h in range(2):
        logits(x, 3, h)
    own_ph.wait()
    ph_copy.wait_recv()
    project(x)

    for copy in g_sum:
        copy.wait_recv()
    gfull[x, mine] = gpart[x, mine] + grecv[0] + grecv[1] + grecv[2]
    g_all = [
        send(gfull.at[x, mine], gfull.at[x, mine], peer(dx=d)) for d in range(1, NX)
    ]
    hops = both_ways(hops, 3, (0, 1))
    for copy in loads[7:]:
        copy.wait()
    id_cols = [jnp.broadcast_to(ids[k], (rows, rows)).T for k in range(3)]
    target = id_cols[0][:, 0:1]
    for copy in g_all:
        copy.wait_recv()
    g_sib = send(gfull.at[:, mine], gfull.at[:, mine], sibling)

    for copies in hops[0]:
        copies.wait_recv()
    logits(xo, 0, 0)
    a_r = send(part.at[0, 0], recv_a.at[0], right)
    logits(xo, 0, 1)
    a_l = send(part.at[0, 1], recv_a.at[1], left)
    for copies in hops[1]:
        copies.wait_recv()
    logits(xl, 2, 0)
    s_l0 = send(part.at[2, 0], recv_b.at[1, 0], left)
    for copies in hops[2]:
        copies.wait_recv()
    logits(xr, 1, 1)
    s_r1 = send(part.at[1, 1], recv_b.at[0, 1], right)
    logits(xl, 2, 1)
    logits(xr, 1, 0)

    own_pv.wait()
    g_sib.wait_recv()
    for q in range(NX):
        cols = pl.ds(q * quarter, quarter)
        g = gfull[q]
        high = g.astype(BF16)
        w[64:128, cols] = high
        w[128:192, cols] = jnp.zeros_like(high)
        w[192:256, cols] = (g - high.astype(F32)).astype(BF16)

    hot = jnp.zeros((rows, 256), F32)
    for h in range(2):
        ids_here = lax.broadcasted_iota(jnp.int32, (rows, half), 1) + (j * vc + h * half)
        onehot = jnp.where(ids_here == target, 1.0, 0.0).astype(BF16)
        hot = hot + dot(onehot, w[:, h * half : (h + 1) * half])
    hot = hot[:, 0:128] + hot[:, 128:256]
    for d in range(NY):
        ve[d, 0:few] = hot[d * few : (d + 1) * few]
    e_sum = [send(ve.at[(y + d) % NY], re.at[d - 1], peer(dy=d)) for d in range(1, NY)]

    a_r.wait_recv()
    part[1, 0] = part[1, 0] + recv_a[0]
    s_r0 = send(part.at[1, 0], recv_b.at[0, 0], right)
    a_l.wait_recv()
    part[2, 1] = part[2, 1] + recv_a[1]
    s_l1 = send(part.at[2, 1], recv_b.at[1, 1], left)

    for chip in blocks:
        project(chip)
    hp_sum = [
        send(hps.at[(x + d) % NX, my_rows], hrecv.at[d - 1], peer(dx=d)) for d in range(1, NX)
    ]

    for copy in e_sum:
        copy.wait_recv()
    vz[...] = ve[y] + sum(re[d] for d in range(NY - 1))
    z_sum = [send(vz, rz.at[z], peer(dz=d)) for d in range(1, NZ)]
    rz[z] = vz[...]
    for copy in hp_sum:
        copy.wait_recv()
    hp = hps[x, my_rows] + hrecv[0] + hrecv[1] + hrecv[2]
    for copy in z_sum:
        copy.wait_recv()
    done = sum(rz[d] for d in range(NZ))
    be[...] = done[0:few]
    my[few : 2 * few] = jnp.where(low, done[few : 2 * few], hp)

    for copy in (s_l0, s_r1, s_r0, s_l1):
        copy.wait_recv()
    vals = [part[3, h] + recv_b[0, h] + recv_b[1, h] for h in range(2)]
    top = jnp.maximum(
        jnp.max(vals[0], axis=1, keepdims=True), jnp.max(vals[1], axis=1, keepdims=True)
    )
    total = jnp.zeros_like(top)
    acc = jnp.zeros((2 * rows, 256), F32)
    for h in range(2):
        e = jnp.exp(vals[h] - top)
        total = total + jnp.sum(e, axis=1, keepdims=True)
        e_high = e.astype(BF16)
        e_low = (e - e_high.astype(F32)).astype(BF16)
        lhs = jnp.concatenate([e_high, e_low], axis=0)
        acc = acc + dot(lhs, w[:, h * half : (h + 1) * half])
    acc = acc[:, 0:128] + acc[:, 128:256]
    soft = acc[0:rows] + acc[rows:]
    stats = jnp.where(low, top, total)
    for d in range(NY):
        at = slice(d * few, (d + 1) * few)
        vy[d, 0:few] = soft[at]
        vy[d, few : 2 * few] = stats[at]

    def combine(parts):
        stats = [p[few : 2 * few] for p in parts]
        tops = [jnp.where(low, s, pltpu.roll(s, 64, 1)) for s in stats]
        best = functools.reduce(jnp.maximum, tops)
        scale = [jnp.exp(t - best) for t in tops]
        value = sum(a * p[0:few] for a, p in zip(scale, parts))
        return value, best, sum(a * s for a, s in zip(scale, stats))

    got = [send(vy.at[(y + d) % NY], ry.at[d - 1], peer(dy=d)) for d in range(1, NY)]
    for copy in got:
        copy.wait_recv()
    value, best, total = combine([vy[y]] + [ry[d] for d in range(NY - 1)])
    vf[0:few] = value
    vf[few : 2 * few] = jnp.where(low, best, total)

    got = [send(vf, rf.at[z], peer(dz=d)) for d in range(1, NZ)]
    rf[z] = vf[...]
    for copy in got:
        copy.wait_recv()
    value, best, total = combine([rf[d] for d in range(NZ)])
    my[0:few] = value / jnp.where(low, pltpu.roll(total, 64, 1), total) - be[...]

    got = [send(my, ay.at[y], peer(dy=d)) for d in range(1, NY)]
    ay[y] = my[...]
    for copy in got:
        copy.wait_recv()
    grads = jnp.concatenate([ay[d, 0:few] for d in range(NY)], axis=0)
    feats = jnp.concatenate([ay[d, few : 2 * few] for d in range(NY)], axis=0)
    factor = (rows * NX * NC) ** -0.5
    grads = grads * (id_cols[1].astype(F32) * factor)
    lhs = jnp.concatenate(
        [jnp.where(id_cols[2] == e, feats, 0.0) for e in range(EXAMPLES)], axis=1
    )
    outer = lax.dot_general(
        lhs, grads, TN, precision=lax.Precision.HIGHEST, preferred_element_type=F32
    )
    for e in range(EXAMPLES):
        feat[64 * e : 64 * e + 64, :] = jnp.where(
            low, outer[128 * e + 64 : 128 * e + 128], outer[128 * e : 128 * e + 64]
        )

    got = [send(feat, rc.at[i], peer(dx, dc)) for dx, dc in ctx_peers]
    rc[i] = feat[...]
    for copy in got:
        copy.wait_recv()
    whole[...] = sum(rc[k] for k in range(NX * NC))
    m = 32
    for e in range(EXAMPLES):
        even = whole[pl.ds(64 * e, m, stride=2), :]
        odd = whole[pl.ds(64 * e + 1, m, stride=2), :]
        out[0, e] = jnp.where(low, even, pltpu.roll(odd, 64, 1))
        out[1, e] = jnp.where(low, pltpu.roll(even, 64, 1), odd)

    for copy in started:
        copy.wait_send()


def local(
    hidden, head, targets, loss_mask, example_ids, down_input, proj_hidden, proj_vocab, proj_grad,
    proj_act,
):
    rows = hidden.shape[0]
    dm, vc = head.shape
    rank = proj_hidden.shape[1]
    half, quarter = vc // 2, vc // NX
    pair = (2 * rows // NY, 128)
    vmem = pl.BlockSpec(memory_space=pltpu.VMEM)
    hbm = pl.BlockSpec(memory_space=pltpu.HBM)
    out = pl.pallas_call(
        kernel,
        out_shape=jax.ShapeDtypeStruct((2, EXAMPLES, 32, 128), F32),
        in_specs=[hbm] * 10,
        out_specs=vmem,
        scratch_shapes=[
            pltpu.VMEM((3, 1, rows), jnp.int32),
            pltpu.VMEM(down_input.shape[::-1], BF16),
            pltpu.VMEM(proj_act.shape[::-1], BF16),
            pltpu.VMEM((NC, dm, vc), BF16),
            pltpu.VMEM((NX, rows, NC * dm), BF16),
            pltpu.VMEM((NC, rank, dm), BF16),
            pltpu.VMEM((NC, rank, dm), BF16),
            pltpu.VMEM((NX, rank, quarter), F32),
            pltpu.VMEM((NX - 1, rank // NC, quarter), F32),
            pltpu.VMEM((NX, rank, quarter), F32),
            pltpu.VMEM((NX, rows, 128), F32),
            pltpu.VMEM((NX - 1, rows // NY, 128), F32),
            pltpu.VMEM((4, 2, rows, half), F32),
            pltpu.VMEM((2, rows, half), F32),
            pltpu.VMEM((2, 2, rows, half), F32),
            pltpu.VMEM((256, vc), BF16),
            pltpu.VMEM((NY,) + pair, F32),
            pltpu.VMEM((NY - 1,) + pair, F32),
            pltpu.VMEM(pair, F32),
            pltpu.VMEM((NZ,) + pair, F32),
            pltpu.VMEM((rows // NY, 128), F32),
            pltpu.VMEM((NY,) + pair, F32),
            pltpu.VMEM((NY - 1,) + pair, F32),
            pltpu.VMEM(pair, F32),
            pltpu.VMEM((NZ,) + pair, F32),
            pltpu.VMEM(pair, F32),
            pltpu.VMEM((NY,) + pair, F32),
            pltpu.VMEM((64 * EXAMPLES, 128), F32),
            pltpu.VMEM((NX * NC, 64 * EXAMPLES, 128), F32),
            pltpu.VMEM((64 * EXAMPLES, 128), F32),
            pltpu.SemaphoreType.DMA((10,)),
            pltpu.SemaphoreType.DMA((COPIES,)),
            pltpu.SemaphoreType.DMA((COPIES,)),
        ],
        compiler_params=pltpu.CompilerParams(
            collective_id=0, has_side_effects=True, vmem_limit_bytes=63 * 2**20
        ),
        name="features",
    )(
        hidden, head, targets.reshape(1, rows), loss_mask.reshape(1, rows),
        example_ids.reshape(1, rows), down_input.T, proj_hidden.T, proj_vocab.T, proj_grad.T,
        proj_act.T,
    )
    return out[0].reshape(EXAMPLES, rank * rank), out[1].reshape(EXAMPLES, rank * rank)


def solution(mesh):
    return jax.shard_map(
        local,
        mesh=mesh,
        in_specs=(
            P("ctx", None),
            P("ctx", "vocab"),
            P("ctx"),
            P("ctx"),
            P("ctx"),
            P("ctx", "vocab"),
            P("ctx", None),
            P("vocab", None),
            P("ctx", None),
            P("vocab", None),
        ),
        out_specs=(P(), P()),
        check_vma=False,
    )
```

```python
import functools

import jax
import jax.numpy as jnp
from jax import lax
from jax.experimental import pallas as pl
from jax.experimental.pallas import tpu as pltpu
from jax.sharding import PartitionSpec as P

MESH = pl.DeviceIdType.MESH
NX, NC, NY, NZ = 4, 2, 8, 8
EXAMPLES = 2
COPIES = 86
STEPS = 32767.0
NT = (((1,), (1,)), ((), ()))
TN = (((0,), (0,)), ((), ()))
F32, BF16 = jnp.float32, jnp.bfloat16


def kernel(
    hidden, head, targets, mask, examples, down_input, ph, pv, pg, pa,
    out_head, out_down,
    ids, di, pac, heads, hid, pgs, phs, away, gpart, grecv, gfull, hps, hrecv,
    part, steps, sizes, got_steps, got_sizes, w, ve, re, vz, rz, be, vy, ry, vf, rf, my, ay, ma, aa, feat, rs, mc, rc, whole,
    lsem, ssem, rsem,
):
    i, j = lax.axis_index("ctx"), lax.axis_index("vocab")
    x, c = i // NC, i % NC
    z, y = j // NY, j % NY

    def peer(dx=0, dc=0, dy=0, dz=0):
        return (
            ((x + dx) % NX) * NC + (c + dc) % NC,
            ((z + dz) % NZ) * NY + (y + dy) % NY,
        )

    ctx_peers = [(dx, dc) for dx in range(NX) for dc in range(NC) if dx or dc]
    started = []

    def send(src, dst, to):
        k = len(started)
        copy = pltpu.make_async_remote_copy(
            src_ref=src, dst_ref=dst, send_sem=ssem.at[k], recv_sem=rsem.at[k],
            device_id=to, device_id_type=MESH,
        )
        copy.start()
        started.append(copy)
        return copy

    def dot(a, b, dims=NT):
        return lax.dot_general(a, b, dims, preferred_element_type=F32)

    dm = heads.shape[1]
    wide = NC * dm
    vc = heads.shape[2]
    half = vc // 2
    rows = hid.shape[1]
    few = rows // NY
    low = lax.broadcasted_iota(jnp.int32, (1, 128), 1) < 64

    def columns_of(chip):
        return pl.ds(pl.multiple_of(chip * wide, 128), wide)

    right, left = peer(dx=1), peer(dx=NX - 1)
    up, down = peer(dy=1), peer(dy=NY - 1)
    sibling = peer(dc=1)
    xr, xl, xo = (x + 1) % NX, (x + NX - 1) % NX, (x + 2) % NX

    barrier = pltpu.get_barrier_semaphore()
    greeted = [peer(dx=2), right, left, sibling, up, down]
    greeted += [peer(dz=d) for d in range(1, NZ)]
    for device in greeted:
        pl.semaphore_signal(barrier, inc=1, device_id=device, device_id_type=MESH)

    loads = [
        pltpu.make_async_copy(src, dst, lsem.at[k])
        for k, (src, dst) in enumerate([
            (head, heads.at[c]),
            (hidden.at[:, columns_of(x)], hid.at[x]),
            (hidden.at[:, columns_of(xo)], away.at[0]),
            (hidden.at[:, columns_of(xr)], away.at[1]),
            (hidden.at[:, columns_of(xl)], away.at[2]),
            (pg, pgs.at[c]),
            (ph, phs.at[c]),
            (pv, w.at[pl.ds(0, 64)]),
            (down_input, di),
            (pa, pac),
            (targets, ids.at[0]),
            (mask, ids.at[1]),
            (examples, ids.at[2]),
        ])
    ]
    for copy in loads:
        copy.start()
    own_head, own_hid, *own_away, own_pg, own_ph, own_pv, own_di, own_pa = loads[:10]

    pl.semaphore_wait(barrier, len(greeted))

    def slab(chip, dy, piece=None):
        at = pl.ds(pl.multiple_of(((y + dy) % NY) * few, few), few)
        if piece is None:
            return hid.at[chip, at]
        return hid.at[chip, at, pl.ds(piece * dm, dm)]

    my_rows = pl.ds(pl.multiple_of(y * few, few), few)
    blocks = (xo,)
    for copy in own_away:
        copy.wait()
    shares = [send(away.at[0, my_rows], hid.at[x, my_rows], peer(dx=2))]
    def both_ways(arrived, dy, pieces=(None, None)):
        moved = []
        for (from_down, from_up), chip in zip(arrived, blocks):
            from_down.wait_recv()
            going_up = slab(chip, -dy, pieces[0])
            moved_up = send(going_up, going_up, up)
            if from_up is not from_down:
                from_up.wait_recv()
            going_down = slab(chip, dy, pieces[1])
            moved.append((moved_up, send(going_down, going_down, down)))
        return moved

    hops = both_ways([(copy, copy) for copy in shares], 0)
    hid_r = send(away.at[1], hid.at[x], right)
    hid_l = send(away.at[2], hid.at[x], left)
    own_head.wait()
    head_copy = send(heads.at[c], heads.at[c], sibling)
    own_pg.wait()
    pg_copy = send(pgs.at[c], pgs.at[c], sibling)
    own_ph.wait()
    ph_copy = send(phs.at[c], phs.at[c], sibling)

    own_di.wait()
    own_pa.wait()
    act_t = dot(pac[...], di[...], (((1,), (0,)), ((), ())))
    act = jnp.concatenate([act_t, act_t], axis=0).T
    for d in range(NY):
        ve[d, few : 2 * few] = act[d * few : (d + 1) * few]

    head_copy.wait_recv()
    pg_copy.wait_recv()
    hops = both_ways(hops, 1)
    quarter = vc // NX
    for q in range(NX):
        cols = pl.ds(q * quarter, quarter)
        gpart[q] = sum(
            dot(pgs[k], heads[k, :, cols], (((1,), (0,)), ((), ()))) for k in range(NC)
        )
    share = gpart.shape[1] // NC
    mine = pl.ds(pl.multiple_of(c * share, 8), share)
    g_sum = [
        send(gpart.at[(x + d) % NX, mine], grecv.at[d - 1], peer(dx=d)) for d in range(1, NX)
    ]

    def logits(chip, h):
        cols = pl.ds(h * half, half)
        return sum(
            dot(
                hid[chip, :, k * dm : (k + 1) * dm], heads[k, :, cols],
                (((1,), (0,)), ((), ())),
            )
            for k in range(NC)
        )

    def project(chip):
        hp = sum(dot(hid[chip, :, k * dm : (k + 1) * dm], phs[k]) for k in range(NC))
        hps[chip] = jnp.concatenate([hp, hp], axis=1)

    def pass_on(value, k, to, where):
        largest = jnp.maximum(jnp.max(jnp.abs(value), axis=1, keepdims=True), 1e-30)
        steps[k] = jnp.round(value * (STEPS / largest)).astype(jnp.int32).astype(jnp.int16)
        sizes[k] = jnp.broadcast_to(largest * (1.0 / STEPS), (rows, 128)).T[0:8]
        return (
            send(steps.at[k], got_steps.at[where], to),
            send(sizes.at[k], got_sizes.at[where], to),
        )

    def passed(copies, where):
        for copy in copies:
            copy.wait_recv()
        size = jnp.broadcast_to(got_sizes[where, 0:1], (128, rows)).T[:, 0:1]
        return got_steps[where].astype(jnp.int32).astype(F32) * size

    own_hid.wait()
    hops = both_ways(hops, 2)
    for h in range(2):
        part[0, h] = logits(x, h)
    ph_copy.wait_recv()
    project(x)

    for copy in g_sum:
        copy.wait_recv()
    gfull[x, mine] = gpart[x, mine] + grecv[0] + grecv[1] + grecv[2]
    g_all = [
        send(gfull.at[x, mine], gfull.at[x, mine], peer(dx=d)) for d in range(1, NX)
    ]
    hops = both_ways(hops, 3, (0, 1))
    for copy in loads[10:]:
        copy.wait()
    id_cols = [jnp.broadcast_to(ids[k], (rows, rows)).T for k in range(3)]
    target = id_cols[0][:, 0:1]
    for copy in g_all:
        copy.wait_recv()
    g_sib = send(gfull.at[:, mine], gfull.at[:, mine], sibling)

    for copies in hops[0]:
        copies.wait_recv()
    a_r = pass_on(logits(xo, 0), 0, right, 0)
    a_l = pass_on(logits(xo, 1), 1, left, 1)
    hid_r.wait_recv()
    s_l0 = pass_on(logits(xl, 0), 2, left, 2)
    hid_l.wait_recv()
    s_r1 = pass_on(logits(xr, 1), 3, right, 3)
    part[1, 1] = logits(xl, 1)
    part[1, 0] = logits(xr, 0)

    own_pv.wait()
    g_sib.wait_recv()
    for q in range(NX):
        cols = pl.ds(q * quarter, quarter)
        g = gfull[q]
        high = g.astype(BF16)
        w[64:128, cols] = high
        w[128:192, cols] = jnp.zeros_like(high)
        w[192:256, cols] = (g - high.astype(F32)).astype(BF16)

    hot = jnp.zeros((rows, 256), F32)
    for h in range(2):
        ids_here = lax.broadcasted_iota(jnp.int32, (rows, half), 1) + (j * vc + h * half)
        onehot = jnp.where(ids_here == target, 1.0, 0.0).astype(BF16)
        hot = hot + dot(onehot, w[:, h * half : (h + 1) * half])
    hot = hot[:, 0:128] + hot[:, 128:256]
    for d in range(NY):
        ve[d, 0:few] = hot[d * few : (d + 1) * few]
    e_sum = [send(ve.at[(y + d) % NY], re.at[d - 1], peer(dy=d)) for d in range(1, NY)]

    s_r0 = pass_on(part[1, 0] + passed(a_r, 0), 4, right, 4)
    s_l1 = pass_on(part[1, 1] + passed(a_l, 1), 5, left, 5)
    part[0, 0] = part[0, 0] + passed(s_l0, 2)
    part[0, 1] = part[0, 1] + passed(s_r1, 3)

    for chip in (xl, xr, xo):
        project(chip)
    hp_sum = [
        send(hps.at[(x + d) % NX, my_rows], hrecv.at[d - 1], peer(dx=d)) for d in range(1, NX)
    ]

    for copy in e_sum:
        copy.wait_recv()
    vz[...] = ve[y] + sum(re[d] for d in range(NY - 1))
    z_sum = [send(vz, rz.at[z], peer(dz=d)) for d in range(1, NZ)]
    rz[z] = vz[...]

    vals = [part[0, 0] + passed(s_r0, 4), part[0, 1] + passed(s_l1, 5)]
    top = jnp.maximum(
        jnp.max(vals[0], axis=1, keepdims=True), jnp.max(vals[1], axis=1, keepdims=True)
    )
    total = jnp.zeros_like(top)
    acc = jnp.zeros((2 * rows, 256), F32)
    for h in range(2):
        e = jnp.exp(vals[h] - top)
        total = total + jnp.sum(e, axis=1, keepdims=True)
        e_high = e.astype(BF16)
        e_low = (e - e_high.astype(F32)).astype(BF16)
        lhs = jnp.concatenate([e_high, e_low], axis=0)
        acc = acc + dot(lhs, w[:, h * half : (h + 1) * half])
    acc = acc[:, 0:128] + acc[:, 128:256]
    soft = acc[0:rows] + acc[rows:]
    lane = lax.broadcasted_iota(jnp.int32, (1, 128), 1)
    fold = few // 2

    def pack(top, total):
        first = jnp.where(lane < 32, top[:fold], total[:fold])
        second = jnp.where(lane < 96, top[fold:], total[fold:])
        return jnp.where(low, first, second)

    def unpack(packed, at):
        wide_of = [jnp.broadcast_to(packed[:, at + k : at + k + 1], (fold, 128)) for k in (0, 64)]
        return jnp.concatenate(wide_of, axis=0)

    for d in range(NY):
        at = slice(d * few, (d + 1) * few)
        vy[d, 0:few] = soft[at]
        vy[d, few:] = pack(top[at], total[at])

    def combine(parts):
        tops = [unpack(p[few:], 0) for p in parts]
        best = functools.reduce(jnp.maximum, tops)
        scale = [jnp.exp(t - best) for t in tops]
        value = sum(a * p[0:few] for a, p in zip(scale, parts))
        return value, best, sum(a * unpack(p[few:], 32) for a, p in zip(scale, parts))

    got = [send(vy.at[(y + d) % NY], ry.at[d - 1], peer(dy=d)) for d in range(1, NY)]
    for copy in hp_sum:
        copy.wait_recv()
    hp = hps[x, my_rows] + hrecv[0] + hrecv[1] + hrecv[2]
    for copy in z_sum:
        copy.wait_recv()
    done = sum(rz[d] for d in range(NZ))
    be[...] = done[0:few]
    ma[...] = jnp.where(low, done[few : 2 * few], hp)
    a_all = [send(ma, aa.at[y], peer(dy=d)) for d in range(1, NY)]
    aa[y] = ma[...]
    for copy in got:
        copy.wait_recv()
    value, best, total = combine([vy[y]] + [ry[d] for d in range(NY - 1)])
    vf[0:few] = value
    vf[few:] = pack(best, total)

    got = [send(vf, rf.at[z], peer(dz=d)) for d in range(1, NZ)]
    rf[z] = vf[...]
    for copy in got:
        copy.wait_recv()
    value, best, total = combine([rf[d] for d in range(NZ)])
    my[...] = value / total - be[...]

    got = [send(my, ay.at[y], peer(dy=d)) for d in range(1, NY)]
    ay[y] = my[...]
    for copy in got:
        copy.wait_recv()
    for copy in a_all:
        copy.wait_recv()
    grads = jnp.concatenate([ay[d] for d in range(NY)], axis=0)
    feats = jnp.concatenate([aa[d] for d in range(NY)], axis=0)
    factor = (rows * NX * NC) ** -0.5
    grads = grads * (id_cols[1].astype(F32) * factor)
    lhs = jnp.concatenate(
        [jnp.where(id_cols[2] == e, feats, 0.0) for e in range(EXAMPLES)], axis=1
    )
    outer = lax.dot_general(
        lhs, grads, TN, precision=lax.Precision.HIGHEST, preferred_element_type=F32
    )
    for e in range(EXAMPLES):
        feat[64 * e : 64 * e + 64, :] = jnp.where(
            low, outer[128 * e + 64 : 128 * e + 128], outer[128 * e : 128 * e + 64]
        )

    hf = 32 * EXAMPLES
    other = send(feat.at[pl.ds(pl.multiple_of((1 - c) * hf, 8), hf)], rs, sibling)
    other.wait_recv()
    mc[...] = feat[pl.ds(pl.multiple_of(c * hf, 8), hf), :] + rs[...]
    got = [send(mc, rc.at[x, c], peer(dx, dc)) for dx, dc in ctx_peers]
    rc[x, c] = mc[...]
    for copy in got:
        copy.wait_recv()
    for k in range(NC):
        whole[k * hf : (k + 1) * hf, :] = sum(rc[chip, k] for chip in range(NX))
    m = 32
    for e in range(EXAMPLES):
        even = whole[pl.ds(64 * e, m, stride=2), :]
        odd = whole[pl.ds(64 * e + 1, m, stride=2), :]
        out_head[e] = jnp.where(low, even, pltpu.roll(odd, 64, 1))
        out_down[e] = jnp.where(low, pltpu.roll(even, 64, 1), odd)

    for copy in started:
        copy.wait_send()


def local(
    hidden, head, targets, loss_mask, example_ids, down_input, proj_hidden, proj_vocab, proj_grad,
    proj_act,
):
    rows = hidden.shape[0]
    dm, vc = head.shape
    rank = proj_hidden.shape[1]
    half, quarter = vc // 2, vc // NX
    pair = (2 * rows // NY, 128)
    packed = (3 * rows // (2 * NY), 128)
    vmem = pl.BlockSpec(memory_space=pltpu.VMEM)
    hbm = pl.BlockSpec(memory_space=pltpu.HBM)
    head_features, down_features = pl.pallas_call(
        kernel,
        out_shape=[jax.ShapeDtypeStruct((EXAMPLES, 32, 128), F32)] * 2,
        in_specs=[hbm] * 10,
        out_specs=[vmem] * 2,
        scratch_shapes=[
            pltpu.VMEM((3, 1, rows), jnp.int32),
            pltpu.VMEM(down_input.shape[::-1], BF16),
            pltpu.VMEM(proj_act.shape[::-1], BF16),
            pltpu.VMEM((NC, dm, vc), BF16),
            pltpu.VMEM((NX, rows, NC * dm), BF16),
            pltpu.VMEM((NC, rank, dm), BF16),
            pltpu.VMEM((NC, rank, dm), BF16),
            pltpu.VMEM((NX - 1, rows, NC * dm), BF16),
            pltpu.VMEM((NX, rank, quarter), F32),
            pltpu.VMEM((NX - 1, rank // NC, quarter), F32),
            pltpu.VMEM((NX, rank, quarter), F32),
            pltpu.VMEM((NX, rows, 128), F32),
            pltpu.VMEM((NX - 1, rows // NY, 128), F32),
            pltpu.VMEM((2, 2, rows, half), F32),
            pltpu.VMEM((6, rows, half), jnp.int16),
            pltpu.VMEM((6, 8, 128), F32),
            pltpu.VMEM((6, rows, half), jnp.int16),
            pltpu.VMEM((6, 8, 128), F32),
            pltpu.VMEM((256, vc), BF16),
            pltpu.VMEM((NY,) + pair, F32),
            pltpu.VMEM((NY - 1,) + pair, F32),
            pltpu.VMEM(pair, F32),
            pltpu.VMEM((NZ,) + pair, F32),
            pltpu.VMEM((rows // NY, 128), F32),
            pltpu.VMEM((NY,) + packed, F32),
            pltpu.VMEM((NY - 1,) + packed, F32),
            pltpu.VMEM(packed, F32),
            pltpu.VMEM((NZ,) + packed, F32),
            pltpu.VMEM((rows // NY, 128), F32),
            pltpu.VMEM((NY, rows // NY, 128), F32),
            pltpu.VMEM((rows // NY, 128), F32),
            pltpu.VMEM((NY, rows // NY, 128), F32),
            pltpu.VMEM((64 * EXAMPLES, 128), F32),
            pltpu.VMEM((32 * EXAMPLES, 128), F32),
            pltpu.VMEM((32 * EXAMPLES, 128), F32),
            pltpu.VMEM((NX, NC, 32 * EXAMPLES, 128), F32),
            pltpu.VMEM((64 * EXAMPLES, 128), F32),
            pltpu.SemaphoreType.DMA((13,)),
            pltpu.SemaphoreType.DMA((COPIES,)),
            pltpu.SemaphoreType.DMA((COPIES,)),
        ],
        compiler_params=pltpu.CompilerParams(
            collective_id=0, has_side_effects=True, vmem_limit_bytes=63 * 2**20
        ),
        name="features",
    )(
        hidden, head, targets.reshape(1, rows), loss_mask.reshape(1, rows),
        example_ids.reshape(1, rows), down_input.T, proj_hidden.T, proj_vocab.T, proj_grad.T,
        proj_act.T,
    )
    return tuple(f.reshape(EXAMPLES, rank * rank) for f in (head_features, down_features))


def solution(mesh):
    return jax.shard_map(
        local,
        mesh=mesh,
        in_specs=(
            P("ctx", None),
            P("ctx", "vocab"),
            P("ctx"),
            P("ctx"),
            P("ctx"),
            P("ctx", "vocab"),
            P("ctx", None),
            P("vocab", None),
            P("ctx", None),
            P("vocab", None),
        ),
        out_specs=(P(), P()),
        check_vma=False,
    )
```

```python
import functools

import jax
import jax.numpy as jnp
from jax import lax
from jax.experimental import pallas as pl
from jax.experimental.pallas import tpu as pltpu
from jax.sharding import PartitionSpec as P

MESH = pl.DeviceIdType.MESH
NX, NC, NY, NZ = 4, 2, 8, 8
EXAMPLES = 2
COPIES = 86
STEPS = 32767.0
NT = (((1,), (1,)), ((), ()))
TN = (((0,), (0,)), ((), ()))
F32, BF16 = jnp.float32, jnp.bfloat16


def kernel(
    hidden, head, targets, mask, examples, down_input, ph, pv, pg, pa,
    out_head, out_down,
    ids, di, pac, heads, hid, pgs, phs, away, gpart, grecv, gfull, hps, hrecv,
    part, steps, sizes, got_steps, got_sizes, w, ve, re, vz, rz, be, vy, ry, vf, rf, my, ay, ma, aa, feat, rs, mc, rc, whole,
    lsem, ssem, rsem,
):
    i, j = lax.axis_index("ctx"), lax.axis_index("vocab")
    x, c = i // NC, i % NC
    z, y = j // NY, j % NY

    def peer(dx=0, dc=0, dy=0, dz=0):
        return (
            ((x + dx) % NX) * NC + (c + dc) % NC,
            ((z + dz) % NZ) * NY + (y + dy) % NY,
        )

    ctx_peers = [(dx, dc) for dx in range(NX) for dc in range(NC) if dx or dc]
    started = []

    def send(src, dst, to):
        k = len(started)
        copy = pltpu.make_async_remote_copy(
            src_ref=src, dst_ref=dst, send_sem=ssem.at[k], recv_sem=rsem.at[k],
            device_id=to, device_id_type=MESH,
        )
        copy.start()
        started.append(copy)
        return copy

    def dot(a, b, dims=NT):
        return lax.dot_general(a, b, dims, preferred_element_type=F32)

    dm = heads.shape[1]
    wide = NC * dm
    vc = heads.shape[2]
    half = vc // 2
    rows = hid.shape[1]
    few = rows // NY
    low = lax.broadcasted_iota(jnp.int32, (1, 128), 1) < 64

    def columns_of(chip):
        return pl.ds(pl.multiple_of(chip * wide, 128), wide)

    right, left = peer(dx=1), peer(dx=NX - 1)
    up, down = peer(dy=1), peer(dy=NY - 1)
    sibling = peer(dc=1)
    xr, xl, xo = (x + 1) % NX, (x + NX - 1) % NX, (x + 2) % NX

    barrier = pltpu.get_barrier_semaphore()
    greeted = [peer(dx=2), right, left, sibling, up, down]
    greeted += [peer(dz=d) for d in range(1, NZ)]
    for device in greeted:
        pl.semaphore_signal(barrier, inc=1, device_id=device, device_id_type=MESH)

    loads = [
        pltpu.make_async_copy(src, dst, lsem.at[k])
        for k, (src, dst) in enumerate([
            (head, heads.at[c]),
            (hidden.at[:, columns_of(x)], hid.at[x]),
            (hidden.at[:, columns_of(xo)], away.at[0]),
            (hidden.at[:, columns_of(xr)], away.at[1]),
            (hidden.at[:, columns_of(xl)], away.at[2]),
            (pg, pgs.at[c]),
            (ph, phs.at[c]),
            (pv, w.at[pl.ds(0, 64)]),
            (down_input, di),
            (pa, pac),
            (targets, ids.at[0]),
            (mask, ids.at[1]),
            (examples, ids.at[2]),
        ])
    ]
    for copy in loads:
        copy.start()
    own_head, own_hid, *own_away, own_pg, own_ph, own_pv, own_di, own_pa = loads[:10]

    pl.semaphore_wait(barrier, len(greeted))

    def slab(chip, dy, piece=None):
        at = pl.ds(pl.multiple_of(((y + dy) % NY) * few, few), few)
        if piece is None:
            return hid.at[chip, at]
        return hid.at[chip, at, pl.ds(piece * dm, dm)]

    my_rows = pl.ds(pl.multiple_of(y * few, few), few)
    blocks = (xo,)
    for copy in own_away:
        copy.wait()
    shares = [send(away.at[0, my_rows], hid.at[x, my_rows], peer(dx=2))]
    hid_r = send(away.at[1], hid.at[x], right)
    hid_l = send(away.at[2], hid.at[x], left)

    def both_ways(arrived, dy, pieces=(None, None)):
        moved = []
        for (from_down, from_up), chip in zip(arrived, blocks):
            from_down.wait_recv()
            going_up = slab(chip, -dy, pieces[0])
            moved_up = send(going_up, going_up, up)
            if from_up is not from_down:
                from_up.wait_recv()
            going_down = slab(chip, dy, pieces[1])
            moved.append((moved_up, send(going_down, going_down, down)))
        return moved

    hops = both_ways([(copy, copy) for copy in shares], 0)
    own_head.wait()
    head_copy = send(heads.at[c], heads.at[c], sibling)
    own_pg.wait()
    pg_copy = send(pgs.at[c], pgs.at[c], sibling)
    own_ph.wait()
    ph_copy = send(phs.at[c], phs.at[c], sibling)

    own_di.wait()
    own_pa.wait()
    act_t = dot(pac[...], di[...], (((1,), (0,)), ((), ())))
    act = jnp.concatenate([act_t, act_t], axis=0).T
    for d in range(NY):
        ve[d, few : 2 * few] = act[d * few : (d + 1) * few]

    head_copy.wait_recv()
    pg_copy.wait_recv()
    hops = both_ways(hops, 1)
    quarter = vc // NX
    for q in range(NX):
        cols = pl.ds(q * quarter, quarter)
        gpart[q] = sum(
            dot(pgs[k], heads[k, :, cols], (((1,), (0,)), ((), ()))) for k in range(NC)
        )
    share = gpart.shape[1] // NC
    mine = pl.ds(pl.multiple_of(c * share, 8), share)
    g_sum = [
        send(gpart.at[(x + d) % NX, mine], grecv.at[d - 1], peer(dx=d)) for d in range(1, NX)
    ]

    def logits(chip, h):
        cols = pl.ds(h * half, half)
        return sum(
            dot(
                hid[chip, :, k * dm : (k + 1) * dm], heads[k, :, cols],
                (((1,), (0,)), ((), ())),
            )
            for k in range(NC)
        )

    def project(chip):
        hp = sum(dot(hid[chip, :, k * dm : (k + 1) * dm], phs[k]) for k in range(NC))
        hps[chip] = jnp.concatenate([hp, hp], axis=1)

    def pass_on(value, k, to, where):
        largest = jnp.maximum(jnp.max(jnp.abs(value), axis=1, keepdims=True), 1e-30)
        steps[k] = jnp.round(value * (STEPS / largest)).astype(jnp.int32).astype(jnp.int16)
        sizes[k] = jnp.broadcast_to(largest * (1.0 / STEPS), (rows, 128)).T[0:8]
        return (
            send(steps.at[k], got_steps.at[where], to),
            send(sizes.at[k], got_sizes.at[where], to),
        )

    def passed(copies, where):
        for copy in copies:
            copy.wait_recv()
        size = jnp.broadcast_to(got_sizes[where, 0:1], (128, rows)).T[:, 0:1]
        return got_steps[where].astype(jnp.int32).astype(F32) * size

    own_hid.wait()
    hops = both_ways(hops, 2)
    for h in range(2):
        part[0, h] = logits(x, h)
    ph_copy.wait_recv()
    project(x)

    for copy in g_sum:
        copy.wait_recv()
    gfull[x, mine] = gpart[x, mine] + grecv[0] + grecv[1] + grecv[2]
    g_all = [
        send(gfull.at[x, mine], gfull.at[x, mine], peer(dx=d)) for d in range(1, NX)
    ]
    hops = both_ways(hops, 3, (0, 1))
    for copy in loads[10:]:
        copy.wait()
    id_cols = [jnp.broadcast_to(ids[k], (rows, rows)).T for k in range(3)]
    target = id_cols[0][:, 0:1]
    for copy in g_all:
        copy.wait_recv()
    g_sib = send(gfull.at[:, mine], gfull.at[:, mine], sibling)

    for copies in hops[0]:
        copies.wait_recv()
    a_r = pass_on(logits(xo, 0), 0, right, 0)
    a_l = pass_on(logits(xo, 1), 1, left, 1)
    hid_r.wait_recv()
    s_l0 = pass_on(logits(xl, 0), 2, left, 2)
    hid_l.wait_recv()
    s_r1 = pass_on(logits(xr, 1), 3, right, 3)
    part[1, 1] = logits(xl, 1)
    part[1, 0] = logits(xr, 0)

    s_r0 = pass_on(part[1, 0] + passed(a_r, 0), 4, right, 4)
    s_l1 = pass_on(part[1, 1] + passed(a_l, 1), 5, left, 5)
    part[0, 0] = part[0, 0] + passed(s_l0, 2)
    part[0, 1] = part[0, 1] + passed(s_r1, 3)

    for chip in (xl, xr, xo):
        project(chip)
    hp_sum = [
        send(hps.at[(x + d) % NX, my_rows], hrecv.at[d - 1], peer(dx=d)) for d in range(1, NX)
    ]

    own_pv.wait()
    g_sib.wait_recv()
    for q in range(NX):
        cols = pl.ds(q * quarter, quarter)
        g = gfull[q]
        high = g.astype(BF16)
        w[64:128, cols] = high
        w[128:192, cols] = jnp.zeros_like(high)
        w[192:256, cols] = (g - high.astype(F32)).astype(BF16)

    hot = jnp.zeros((rows, 256), F32)
    for h in range(2):
        ids_here = lax.broadcasted_iota(jnp.int32, (rows, half), 1) + (j * vc + h * half)
        onehot = jnp.where(ids_here == target, 1.0, 0.0).astype(BF16)
        hot = hot + dot(onehot, w[:, h * half : (h + 1) * half])
    hot = hot[:, 0:128] + hot[:, 128:256]
    for d in range(NY):
        ve[d, 0:few] = hot[d * few : (d + 1) * few]
    e_sum = [send(ve.at[(y + d) % NY], re.at[d - 1], peer(dy=d)) for d in range(1, NY)]

    vals = [part[0, 0] + passed(s_r0, 4), part[0, 1] + passed(s_l1, 5)]
    top = jnp.maximum(
        jnp.max(vals[0], axis=1, keepdims=True), jnp.max(vals[1], axis=1, keepdims=True)
    )
    total = jnp.zeros_like(top)
    acc = jnp.zeros((2 * rows, 256), F32)
    for h in range(2):
        e = jnp.exp(vals[h] - top)
        total = total + jnp.sum(e, axis=1, keepdims=True)
        e_high = e.astype(BF16)
        e_low = (e - e_high.astype(F32)).astype(BF16)
        lhs = jnp.concatenate([e_high, e_low], axis=0)
        acc = acc + dot(lhs, w[:, h * half : (h + 1) * half])
    acc = acc[:, 0:128] + acc[:, 128:256]
    soft = acc[0:rows] + acc[rows:]
    lane = lax.broadcasted_iota(jnp.int32, (1, 128), 1)
    fold = few // 2

    def pack(top, total):
        first = jnp.where(lane < 32, top[:fold], total[:fold])
        second = jnp.where(lane < 96, top[fold:], total[fold:])
        return jnp.where(low, first, second)

    def unpack(packed, at):
        wide_of = [jnp.broadcast_to(packed[:, at + k : at + k + 1], (fold, 128)) for k in (0, 64)]
        return jnp.concatenate(wide_of, axis=0)

    for d in range(NY):
        at = slice(d * few, (d + 1) * few)
        vy[d, 0:few] = soft[at]
        vy[d, few:] = pack(top[at], total[at])

    def combine(parts):
        tops = [unpack(p[few:], 0) for p in parts]
        best = functools.reduce(jnp.maximum, tops)
        scale = [jnp.exp(t - best) for t in tops]
        value = sum(a * p[0:few] for a, p in zip(scale, parts))
        return value, best, sum(a * unpack(p[few:], 32) for a, p in zip(scale, parts))

    got = [send(vy.at[(y + d) % NY], ry.at[d - 1], peer(dy=d)) for d in range(1, NY)]
    for copy in e_sum:
        copy.wait_recv()
    vz[...] = ve[y] + sum(re[d] for d in range(NY - 1))
    z_sum = [send(vz, rz.at[z], peer(dz=d)) for d in range(1, NZ)]
    rz[z] = vz[...]
    for copy in got:
        copy.wait_recv()
    value, best, total = combine([vy[y]] + [ry[d] for d in range(NY - 1)])
    vf[0:few] = value
    vf[few:] = pack(best, total)

    got = [send(vf, rf.at[z], peer(dz=d)) for d in range(1, NZ)]
    for copy in hp_sum:
        copy.wait_recv()
    hp = hps[x, my_rows] + hrecv[0] + hrecv[1] + hrecv[2]
    for copy in z_sum:
        copy.wait_recv()
    done = sum(rz[d] for d in range(NZ))
    be[...] = done[0:few]
    ma[...] = jnp.where(low, done[few : 2 * few], hp)
    a_all = [send(ma, aa.at[y], peer(dy=d)) for d in range(1, NY)]
    aa[y] = ma[...]
    rf[z] = vf[...]
    for copy in got:
        copy.wait_recv()
    value, best, total = combine([rf[d] for d in range(NZ)])
    my[...] = value / total - be[...]

    got = [send(my, ay.at[y], peer(dy=d)) for d in range(1, NY)]
    ay[y] = my[...]
    for copy in got:
        copy.wait_recv()
    for copy in a_all:
        copy.wait_recv()
    grads = jnp.concatenate([ay[d] for d in range(NY)], axis=0)
    feats = jnp.concatenate([aa[d] for d in range(NY)], axis=0)
    factor = (rows * NX * NC) ** -0.5
    grads = grads * (id_cols[1].astype(F32) * factor)
    lhs = jnp.concatenate(
        [jnp.where(id_cols[2] == e, feats, 0.0) for e in range(EXAMPLES)], axis=1
    )
    outer = lax.dot_general(
        lhs, grads, TN, precision=lax.Precision.HIGHEST, preferred_element_type=F32
    )
    for e in range(EXAMPLES):
        feat[64 * e : 64 * e + 64, :] = jnp.where(
            low, outer[128 * e + 64 : 128 * e + 128], outer[128 * e : 128 * e + 64]
        )

    hf = 32 * EXAMPLES
    other = send(feat.at[pl.ds(pl.multiple_of((1 - c) * hf, 8), hf)], rs, sibling)
    other.wait_recv()
    mc[...] = feat[pl.ds(pl.multiple_of(c * hf, 8), hf), :] + rs[...]
    got = [send(mc, rc.at[x, c], peer(dx, dc)) for dx, dc in ctx_peers]
    rc[x, c] = mc[...]
    for copy in got:
        copy.wait_recv()
    for k in range(NC):
        whole[k * hf : (k + 1) * hf, :] = sum(rc[chip, k] for chip in range(NX))
    m = 32
    for e in range(EXAMPLES):
        even = whole[pl.ds(64 * e, m, stride=2), :]
        odd = whole[pl.ds(64 * e + 1, m, stride=2), :]
        out_head[e] = jnp.where(low, even, pltpu.roll(odd, 64, 1))
        out_down[e] = jnp.where(low, pltpu.roll(even, 64, 1), odd)

    for copy in started:
        copy.wait_send()


def local(
    hidden, head, targets, loss_mask, example_ids, down_input, proj_hidden, proj_vocab, proj_grad,
    proj_act,
):
    rows = hidden.shape[0]
    dm, vc = head.shape
    rank = proj_hidden.shape[1]
    half, quarter = vc // 2, vc // NX
    pair = (2 * rows // NY, 128)
    packed = (3 * rows // (2 * NY), 128)
    vmem = pl.BlockSpec(memory_space=pltpu.VMEM)
    hbm = pl.BlockSpec(memory_space=pltpu.HBM)
    head_features, down_features = pl.pallas_call(
        kernel,
        out_shape=[jax.ShapeDtypeStruct((EXAMPLES, 32, 128), F32)] * 2,
        in_specs=[hbm] * 10,
        out_specs=[vmem] * 2,
        scratch_shapes=[
            pltpu.VMEM((3, 1, rows), jnp.int32),
            pltpu.VMEM(down_input.shape[::-1], BF16),
            pltpu.VMEM(proj_act.shape[::-1], BF16),
            pltpu.VMEM((NC, dm, vc), BF16),
            pltpu.VMEM((NX, rows, NC * dm), BF16),
            pltpu.VMEM((NC, rank, dm), BF16),
            pltpu.VMEM((NC, rank, dm), BF16),
            pltpu.VMEM((NX - 1, rows, NC * dm), BF16),
            pltpu.VMEM((NX, rank, quarter), F32),
            pltpu.VMEM((NX - 1, rank // NC, quarter), F32),
            pltpu.VMEM((NX, rank, quarter), F32),
            pltpu.VMEM((NX, rows, 128), F32),
            pltpu.VMEM((NX - 1, rows // NY, 128), F32),
            pltpu.VMEM((2, 2, rows, half), F32),
            pltpu.VMEM((6, rows, half), jnp.int16),
            pltpu.VMEM((6, 8, 128), F32),
            pltpu.VMEM((6, rows, half), jnp.int16),
            pltpu.VMEM((6, 8, 128), F32),
            pltpu.VMEM((256, vc), BF16),
            pltpu.VMEM((NY,) + pair, F32),
            pltpu.VMEM((NY - 1,) + pair, F32),
            pltpu.VMEM(pair, F32),
            pltpu.VMEM((NZ,) + pair, F32),
            pltpu.VMEM((rows // NY, 128), F32),
            pltpu.VMEM((NY,) + packed, F32),
            pltpu.VMEM((NY - 1,) + packed, F32),
            pltpu.VMEM(packed, F32),
            pltpu.VMEM((NZ,) + packed, F32),
            pltpu.VMEM((rows // NY, 128), F32),
            pltpu.VMEM((NY, rows // NY, 128), F32),
            pltpu.VMEM((rows // NY, 128), F32),
            pltpu.VMEM((NY, rows // NY, 128), F32),
            pltpu.VMEM((64 * EXAMPLES, 128), F32),
            pltpu.VMEM((32 * EXAMPLES, 128), F32),
            pltpu.VMEM((32 * EXAMPLES, 128), F32),
            pltpu.VMEM((NX, NC, 32 * EXAMPLES, 128), F32),
            pltpu.VMEM((64 * EXAMPLES, 128), F32),
            pltpu.SemaphoreType.DMA((13,)),
            pltpu.SemaphoreType.DMA((COPIES,)),
            pltpu.SemaphoreType.DMA((COPIES,)),
        ],
        compiler_params=pltpu.CompilerParams(
            collective_id=0, has_side_effects=True, vmem_limit_bytes=63 * 2**20
        ),
        name="features",
    )(
        hidden, head, targets.reshape(1, rows), loss_mask.reshape(1, rows),
        example_ids.reshape(1, rows), down_input.T, proj_hidden.T, proj_vocab.T, proj_grad.T,
        proj_act.T,
    )
    return tuple(f.reshape(EXAMPLES, rank * rank) for f in (head_features, down_features))


def solution(mesh):
    return jax.shard_map(
        local,
        mesh=mesh,
        in_specs=(
            P("ctx", None),
            P("ctx", "vocab"),
            P("ctx"),
            P("ctx"),
            P("ctx"),
            P("ctx", "vocab"),
            P("ctx", None),
            P("vocab", None),
            P("ctx", None),
            P("vocab", None),
        ),
        out_specs=(P(), P()),
        check_vma=False,
    )
```
